32 devices in a mesh: row: 4 (over y, x), col: 4 (over z), depth: 2 (over core).
Axes of the slice: x: 2, y: 2, z: 4, core: 2. Of those that a mesh axis runs over, the one named last changes fastest.
Arguments:
- tokens: bfloat16 [1024, 8192], P(('col', 'depth'), 'row'), may hold values from -6 to 6
- out_grad: bfloat16 [1024, 8192], P(('col', 'depth'), 'row'), may hold values from -6 to 6
- gate_weight: bfloat16 [8192, 14336], P('row', ('col', 'depth')), may hold values from -0.0625 to 0.0625
- up_weight: bfloat16 [8192, 14336], P('row', ('col', 'depth')), may hold values from -0.0625 to 0.0625
- down_weight: bfloat16 [8192, 14336], P('row', ('col', 'depth')), may hold values from -0.046875 to 0.046875
- gate_mask: int32 [128, 224], P('row', ('col', 'depth')), may hold values 0 or 1
- up_mask: int32 [128, 224], P('row', ('col', 'depth')), may hold values 0 or 1
- down_mask: int32 [128, 224], P('row', ('col', 'depth')), may hold values 0 or 1
Outputs:
- output: float32 [1024, 8192], P(('col', 'depth'), 'row')
- in_grad: float32 [1024, 8192], P(('col', 'depth'), 'row')
- gate_grad: float32 [8192, 14336], P('row', ('col', 'depth'))
- up_grad: float32 [8192, 14336], P('row', ('col', 'depth'))
- down_grad: float32 [8192, 14336], P('row', ('col', 'depth'))
The draws below stay inside these ranges and needn't reach their ends.
All inputs are finite; a program needn't handle non-finite values. No bound on the sum of `gate_mask` or of `up_mask` or of `down_mask` on one device may be relied on, other than what follows from the above.
Results may differ from the reference program's by a relative error of at most 0.0029.
Values may be sent and summed in bfloat16 or wider, within the bound.
A program may use at most 384 MiB of HBM per device.

```python
import jax
import jax.numpy as jnp

D = 8192
FF = 14336
BLOCK = 64
TOKENS = 1024


def plant(drawn, stream_key, low, largest):
    index_at = [jax.random.randint(jax.random.fold_in(stream_key, axis), (), 0, length) for axis, length in enumerate(drawn.shape)]
    widest = drawn.shape.index(max(drawn.shape))
    beside = index_at[:widest] + [(index_at[widest] + 1) % drawn.shape[widest]] + index_at[widest + 1:]
    return drawn.at[tuple(index_at)].set(low).at[tuple(beside)].set(largest)


def block_levels(key, dims, split, least, high):
    def one(axis_at, blocks):
        heights = jax.random.uniform(jax.random.fold_in(jax.random.fold_in(key, 6), axis_at), (blocks,), jnp.float32, least / len(split), high / len(split))
        return jnp.repeat(jnp.exp(heights), dims[axis_at] // blocks).reshape((-1,) + (1,) * (len(dims) - axis_at - 1))

    loudness = one(*split[0])
    for cut in split[1:]:
        loudness = loudness * one(*cut)
    return loudness


def bell_draw(key, dims, width, reach, pieces=(), dtype=jnp.bfloat16):
    values = width * jax.random.normal(key, dims, jnp.float32)
    if pieces:
        values = values * block_levels(key, dims, pieces, -0.22, 0.18)
    return jnp.clip(values, -reach, reach).astype(dtype)


def setup_inputs(seed: int = 0) -> dict:
    streams_of = jax.random.split(jax.random.key(seed), 9)
    tokens = bell_draw(streams_of[0], (TOKENS, D), 1.0, 6.0, ((0, 8), (1, 4)))
    out_grad = bell_draw(streams_of[1], (TOKENS, D), 1.0, 6.0, ((0, 8), (1, 4)))
    gate_weight = bell_draw(streams_of[2], (D, FF), D ** -0.5, 0.0625, ((0, 4), (1, 8)))
    up_weight = bell_draw(streams_of[3], (D, FF), D ** -0.5, 0.0625, ((0, 4), (1, 8)))
    down_weight = bell_draw(streams_of[4], (D, FF), FF ** -0.5, 0.046875, ((0, 4), (1, 8)))
    gate_mask = plant((jax.random.randint(streams_of[5], (D // BLOCK, FF // BLOCK), 0, 2) < 1).astype(jnp.int32), jax.random.fold_in(streams_of[5], 1), 0, 1)
    up_mask = plant((jax.random.randint(streams_of[6], (D // BLOCK, FF // BLOCK), 0, 2) < 1).astype(jnp.int32), jax.random.fold_in(streams_of[6], 1), 0, 1)
    down_mask = plant((jax.random.randint(streams_of[7], (D // BLOCK, FF // BLOCK), 0, 2) < 1).astype(jnp.int32), jax.random.fold_in(streams_of[7], 1), 0, 1)
    return dict(tokens=tokens, out_grad=out_grad, gate_weight=gate_weight, up_weight=up_weight, down_weight=down_weight, gate_mask=gate_mask, up_mask=up_mask, down_mask=down_mask)


def expand(mask):
    return jnp.repeat(jnp.repeat(mask, BLOCK, axis=0), BLOCK, axis=1)


def reference(tokens, out_grad, gate_weight, up_weight, down_weight, gate_mask, up_mask, down_mask):
    mask_gate = expand(gate_mask)
    mask_up = expand(up_mask)
    mask_down = expand(down_mask)
    masked_gate = gate_weight * mask_gate.astype(jnp.bfloat16)
    masked_up = up_weight * mask_up.astype(jnp.bfloat16)
    masked_down = down_weight * mask_down.astype(jnp.bfloat16)
    gate = jnp.dot(tokens, masked_gate, preferred_element_type=jnp.float32)
    up = jnp.dot(tokens, masked_up, preferred_element_type=jnp.float32)
    sig = jax.nn.sigmoid(gate)
    act = gate * sig
    hidden = (act * up).astype(jnp.bfloat16)
    output = jnp.dot(hidden, masked_down.T, preferred_element_type=jnp.float32)
    hidden_grad = jnp.dot(out_grad, masked_down, preferred_element_type=jnp.float32)
    gate_term = (hidden_grad * up * sig * (1.0 + gate * (1.0 - sig))).astype(jnp.bfloat16)
    up_term = (hidden_grad * act).astype(jnp.bfloat16)
    in_grad = jnp.dot(gate_term, masked_gate.T, preferred_element_type=jnp.float32) + jnp.dot(up_term, masked_up.T, preferred_element_type=jnp.float32)
    gate_grad = jnp.dot(tokens.T, gate_term, preferred_element_type=jnp.float32) * mask_gate.astype(jnp.float32)
    up_grad = jnp.dot(tokens.T, up_term, preferred_element_type=jnp.float32) * mask_up.astype(jnp.float32)
    down_grad = jnp.dot(out_grad.T, hidden, preferred_element_type=jnp.float32) * mask_down.astype(jnp.float32)
    return (output, in_grad, gate_grad, up_grad, down_grad)
```

```python
import jax
import jax.numpy as jnp
from jax import lax
from jax.sharding import PartitionSpec as P

SPLIT = 2
F32 = jnp.float32
BF16 = jnp.bfloat16
F16 = jnp.float16
F16_ROOM = 2.0**14


def contract_last(left, right):
    return lax.dot_general(left, right, (((1,), (1,)), ((), ())), preferred_element_type=F32)


def contract_first(left, right):
    return lax.dot_general(left, right, (((0,), (0,)), ((), ())), preferred_element_type=F32)


def wide_columns(mask, block):
    cols = mask.shape[1]
    unit = jnp.arange(cols)[:, None] == (jnp.arange(cols * block) // block)[None, :]
    return jnp.dot(mask.astype(BF16), unit.astype(BF16), preferred_element_type=F32)


def apply_mask(values, wide):
    rows, cols = values.shape
    shaped = values.reshape(wide.shape[0], rows // wide.shape[0], cols)
    return (shaped * wide.astype(values.dtype)[:, None, :]).reshape(rows, cols)


def full_mask(wide, rows):
    count, cols = wide.shape
    spread = jnp.broadcast_to(wide.astype(BF16)[:, None, :], (count, rows // count, cols))
    return lax.optimization_barrier(spread.reshape(rows, cols))


def half_at(values, which):
    count = values.shape[0] // 2
    return lax.dynamic_slice_in_dim(values, which * count, count, 0)


def join_halves(mine, other, which):
    first = jnp.where(which == 0, mine, other)
    second = jnp.where(which == 0, other, mine)
    return jnp.concatenate([first, second], axis=0)


class RowGroup:
    def __init__(self):
        self.size = lax.axis_size("row")
        self.cores = lax.axis_size("depth")
        self.bits = self.size.bit_length() - 1
        assert 1 << self.bits == self.size
        me, core = lax.axis_index("row"), lax.axis_index("depth")
        self.mine = []
        for stage in range(self.bits):
            bit = (stage + core * (self.bits // 2)) % self.bits
            self.mine.append((me >> bit) & 1)

    def swap(self, values, stage):
        pairs = []
        for r in range(self.size):
            for d in range(self.cores):
                bit = (stage + d * (self.bits // 2)) % self.bits
                pairs.append((r * self.cores + d, (r ^ (1 << bit)) * self.cores + d))
        return lax.ppermute(values, ("row", "depth"), pairs)

    def scatter_product(self, left, right, bound):
        scale, back = F16_ROOM / bound, bound / F16_ROOM
        bit = self.mine[0]
        away = jnp.dot(half_at(left, 1 - bit), right, preferred_element_type=F32)
        landed = self.swap((away * scale).astype(F16), 0)
        total = jnp.dot(half_at(left, bit), right, preferred_element_type=F32)
        total = total + landed.astype(F32) * back
        for stage in range(1, self.bits):
            bit = self.mine[stage]
            landed = self.swap((half_at(total, 1 - bit) * scale).astype(F16), stage)
            total = half_at(total, bit) + landed.astype(F32) * back
        return total

    def gather(self, values):
        for stage in reversed(range(self.bits)):
            values = join_halves(values, self.swap(values, stage), self.mine[stage])
        return values


def gather_tokens(values):
    over_col = lax.all_gather(values, "col", axis=0)
    both = lax.all_gather(over_col, "depth", axis=1)
    return both.reshape(-1, values.shape[1])


def scatter_tokens(term):
    cols, cores = lax.axis_size("col"), lax.axis_size("depth")
    assert cores == 2
    core, me = lax.axis_index("depth"), lax.axis_index("col")

    def rows_of(which):
        def select(values):
            shaped = values.reshape(cols, cores, -1, values.shape[1])
            return lax.dynamic_index_in_dim(shaped, which, 1, keepdims=False).reshape(-1, values.shape[1])

        return select

    landed = lax.ppermute(term(rows_of(1 - core)), "depth", [(0, 1), (1, 0)])
    total = term(rows_of(core)) + landed
    width = total.shape[1]
    bits = cols.bit_length() - 1
    assert 1 << bits == cols
    for bit in range(bits):
        side = (me >> bit) & 1
        shaped = total.reshape(cols >> (bit + 1), 2, -1, width)

        def pick(which):
            return lax.dynamic_index_in_dim(shaped, which, 1, keepdims=False).reshape(-1, width)

        pairs = [(c, c ^ (1 << bit)) for c in range(cols)]
        landed = lax.ppermute(pick(1 - side).astype(BF16), "col", pairs)
        total = pick(side) + landed.astype(F32)
    return total


def product_bounds(tokens, out_grad, gate_weight, up_weight, down_weight):
    tops = [jnp.max(jnp.abs(v)).astype(F32) for v in (tokens, out_grad, gate_weight, up_weight, down_weight)]
    tops = lax.pmax(jnp.stack(tops), ("row", "col", "depth"))
    features = tokens.shape[1] * lax.axis_size("row")
    return [
        jnp.maximum(tops[a] * tops[b] * features, 1e-30) for a, b in ((0, 2), (0, 3), (1, 4))
    ]


def per_device(
    tokens, out_grad, gate_weight, up_weight, down_weight, gate_mask, up_mask, down_mask
):
    block = gate_weight.shape[0] // gate_mask.shape[0]
    row = RowGroup()
    own = tokens.shape[0] // SPLIT
    inputs, grads_in = [], []
    for part in range(SPLIT):
        inputs.append(gather_tokens(tokens[part * own : (part + 1) * own]))
        grads_in.append(gather_tokens(out_grad[part * own : (part + 1) * own]))
    gate_bound, up_bound, hidden_bound = product_bounds(
        tokens, out_grad, gate_weight, up_weight, down_weight
    )
    wide_gate = wide_columns(gate_mask, block)
    wide_up = wide_columns(up_mask, block)
    wide_down = wide_columns(down_mask, block)
    w_gate = apply_mask(gate_weight, wide_gate)
    w_up = apply_mask(up_weight, wide_up)
    w_down = apply_mask(down_weight, wide_down)

    rows = gate_weight.shape[0]
    full_gate, full_up, full_down = (
        full_mask(wide_gate, rows),
        full_mask(wide_up, rows),
        full_mask(wide_down, rows),
    )

    hiddens, gate_terms, up_terms, outputs, in_grads = [], [], [], [], []
    for part in range(SPLIT):
        gate = row.scatter_product(inputs[part], w_gate, gate_bound)
        up = row.scatter_product(inputs[part], w_up, up_bound)
        sig = jax.nn.sigmoid(gate)
        act = gate * sig
        hidden = row.gather((act * up).astype(BF16))
        hidden_grad = row.scatter_product(grads_in[part], w_down, hidden_bound)
        gate_term = row.gather((hidden_grad * up * sig * (1.0 + gate * (1.0 - sig))).astype(BF16))
        up_term = row.gather((hidden_grad * act).astype(BF16))
        outputs.append(scatter_tokens(lambda select: contract_last(select(hidden), w_down)))
        in_grads.append(
            scatter_tokens(
                lambda select: contract_last(select(gate_term), w_gate)
                + contract_last(select(up_term), w_up)
            )
        )
        hiddens.append(hidden)
        gate_terms.append(gate_term)
        up_terms.append(up_term)

    def joined(parts):
        return jnp.concatenate(parts, axis=0)

    all_inputs, all_grads = joined(inputs), joined(grads_in)
    gate_grad = contract_first(all_inputs, joined(gate_terms)) * full_gate.astype(F32)
    up_grad = contract_first(all_inputs, joined(up_terms)) * full_up.astype(F32)
    down_grad = contract_first(all_grads, joined(hiddens)) * full_down.astype(F32)
    return (joined(outputs), joined(in_grads), gate_grad, up_grad, down_grad)


def solution(mesh):
    tokens, weights = P(("col", "depth"), "row"), P("row", ("col", "depth"))
    return jax.shard_map(
        per_device,
        mesh=mesh,
        in_specs=(tokens,) * 2 + (weights,) * 6,
        out_specs=(tokens,) * 2 + (weights,) * 3,
        check_vma=False,
    )
```

```python
import jax
import jax.numpy as jnp
from jax import lax
from jax.sharding import PartitionSpec as P

SPLIT = 2
F32 = jnp.float32
BF16 = jnp.bfloat16
F16 = jnp.float16
F16_ROOM = 2.0**14


def contract_last(left, right):
    return lax.dot_general(left, right, (((1,), (1,)), ((), ())), preferred_element_type=F32)


def contract_first(left, right):
    return lax.dot_general(left, right, (((0,), (0,)), ((), ())), preferred_element_type=F32)


def wide_columns(mask, block):
    cols = mask.shape[1]
    unit = jnp.arange(cols)[:, None] == (jnp.arange(cols * block) // block)[None, :]
    return jnp.dot(mask.astype(BF16), unit.astype(BF16), preferred_element_type=F32)


def apply_mask(values, wide):
    rows, cols = values.shape
    shaped = values.reshape(wide.shape[0], rows // wide.shape[0], cols)
    return (shaped * wide.astype(values.dtype)[:, None, :]).reshape(rows, cols)


def full_mask(wide, rows):
    count, cols = wide.shape
    spread = jnp.broadcast_to(wide.astype(BF16)[:, None, :], (count, rows // count, cols))
    return lax.optimization_barrier(spread.reshape(rows, cols))


def half_at(values, which):
    count = values.shape[0] // 2
    return lax.dynamic_slice_in_dim(values, which * count, count, 0)


def join_halves(mine, other, which):
    first = jnp.where(which == 0, mine, other)
    second = jnp.where(which == 0, other, mine)
    return jnp.concatenate([first, second], axis=0)


class RowGroup:
    def __init__(self):
        self.size = lax.axis_size("row")
        self.cores = lax.axis_size("depth")
        self.bits = self.size.bit_length() - 1
        assert 1 << self.bits == self.size
        me, core = lax.axis_index("row"), lax.axis_index("depth")
        self.mine = []
        for stage in range(self.bits):
            bit = (stage + core * (self.bits // 2)) % self.bits
            self.mine.append((me >> bit) & 1)

    def swap(self, values, stage):
        pairs = []
        for r in range(self.size):
            for d in range(self.cores):
                bit = (stage + d * (self.bits // 2)) % self.bits
                pairs.append((r * self.cores + d, (r ^ (1 << bit)) * self.cores + d))
        return lax.ppermute(values, ("row", "depth"), pairs)

    def scatter_product(self, left, right, bound):
        scale, back = F16_ROOM / bound, bound / F16_ROOM
        bit = self.mine[0]
        away = jnp.dot(half_at(left, 1 - bit), right, preferred_element_type=F32)
        landed = self.swap((away * scale).astype(F16), 0)
        total = jnp.dot(half_at(left, bit), right, preferred_element_type=F32)
        total = total + landed.astype(F32) * back
        for stage in range(1, self.bits):
            bit = self.mine[stage]
            landed = self.swap((half_at(total, 1 - bit) * scale).astype(F16), stage)
            total = half_at(total, bit) + landed.astype(F32) * back
        return total

    def gather(self, values):
        for stage in reversed(range(self.bits)):
            values = join_halves(values, self.swap(values, stage), self.mine[stage])
        return values


def after(values, earlier):
    return lax.optimization_barrier((values, earlier))[0]


def swap_cores(values):
    return lax.ppermute(values, "depth", [(0, 1), (1, 0)])


def gather_tokens(values):
    cols, cores = lax.axis_size("col"), lax.axis_size("depth")
    assert cores == 2 and cols & (cols - 1) == 0
    me = lax.axis_index("col")
    blocks = [values[None]]
    for other in range(1, cols):
        pairs = [(c, c ^ other) for c in range(cols)]
        blocks.append(lax.ppermute(values, "col", pairs)[None])
    bit = 0
    while len(blocks) > 1:
        side = (me >> bit) & 1
        blocks = [
            join_halves(blocks[k], blocks[k + 1], side) for k in range(0, len(blocks), 2)
        ]
        bit += 1
    mine = blocks[0]
    other = swap_cores(mine)
    core = lax.axis_index("depth")
    first = jnp.where(core == 0, mine, other)
    second = jnp.where(core == 0, other, mine)
    return jnp.stack([first, second], axis=1).reshape(-1, values.shape[1])


def core_sum(term):
    cols, cores = lax.axis_size("col"), lax.axis_size("depth")
    assert cores == 2
    core = lax.axis_index("depth")

    def rows_of(which):
        def select(values):
            shaped = values.reshape(cols, cores, -1, values.shape[1])
            return lax.dynamic_index_in_dim(shaped, which, 1, keepdims=False).reshape(-1, values.shape[1])

        return select

    landed = swap_cores(term(rows_of(1 - core)))
    return term(rows_of(core)) + landed


def col_stage(total, bit):
    cols, width = lax.axis_size("col"), total.shape[1]
    assert cols & (cols - 1) == 0
    side = (lax.axis_index("col") >> bit) & 1
    shaped = total.reshape(cols >> (bit + 1), 2, -1, width)

    def pick(which):
        return lax.dynamic_index_in_dim(shaped, which, 1, keepdims=False).reshape(-1, width)

    return pick(side), pick(1 - side).astype(BF16)


def col_swap(kept, sent, bit):
    pairs = [(c, c ^ (1 << bit)) for c in range(lax.axis_size("col"))]
    return kept + lax.ppermute(sent, "col", pairs).astype(F32)


def product_bounds(tokens, out_grad, gate_weight, up_weight, down_weight):
    tops = [jnp.max(jnp.abs(v)).astype(F32) for v in (tokens, out_grad, gate_weight, up_weight, down_weight)]
    tops = lax.pmax(jnp.stack(tops), ("row", "col", "depth"))
    features = tokens.shape[1] * lax.axis_size("row")
    return [
        jnp.maximum(tops[a] * tops[b] * features, 1e-30) for a, b in ((0, 2), (0, 3), (1, 4))
    ]


def per_device(
    tokens, out_grad, gate_weight, up_weight, down_weight, gate_mask, up_mask, down_mask
):
    block = gate_weight.shape[0] // gate_mask.shape[0]
    row = RowGroup()
    own = tokens.shape[0] // SPLIT
    inputs, grads_in = [], []
    last = None
    for part in range(SPLIT):
        for source, gathered in ((tokens, inputs), (out_grad, grads_in)):
            rows = source[part * own : (part + 1) * own]
            last = gather_tokens(rows if last is None else after(rows, last))
            gathered.append(last)
    gate_bound, up_bound, hidden_bound = product_bounds(
        tokens, out_grad, gate_weight, up_weight, down_weight
    )
    wide_gate = wide_columns(gate_mask, block)
    wide_up = wide_columns(up_mask, block)
    wide_down = wide_columns(down_mask, block)
    w_gate = apply_mask(gate_weight, wide_gate)
    w_up = apply_mask(up_weight, wide_up)
    w_down = apply_mask(down_weight, wide_down)

    rows = gate_weight.shape[0]
    full_gate, full_up, full_down = (
        full_mask(wide_gate, rows),
        full_mask(wide_up, rows),
        full_mask(wide_down, rows),
    )

    hiddens, gate_terms, up_terms, outputs, in_grads = [], [], [], [], []
    for part in range(SPLIT):
        gate = row.scatter_product(inputs[part], w_gate, gate_bound)
        up = row.scatter_product(inputs[part], w_up, up_bound)
        sig = jax.nn.sigmoid(gate)
        act = gate * sig
        hidden = row.gather((act * up).astype(BF16))
        hidden_grad = row.scatter_product(grads_in[part], w_down, hidden_bound)
        gate_term = row.gather((hidden_grad * up * sig * (1.0 + gate * (1.0 - sig))).astype(BF16))
        up_term = row.gather((hidden_grad * act).astype(BF16))
        outputs.append(core_sum(lambda select: contract_last(select(hidden), w_down)))
        in_grads.append(
            core_sum(
                lambda select: contract_last(select(gate_term), w_gate)
                + contract_last(select(up_term), w_up)
            )
        )
        hiddens.append(hidden)
        gate_terms.append(gate_term)
        up_terms.append(up_term)

    def joined(parts):
        return jnp.concatenate(parts, axis=0)

    all_inputs, all_grads = joined(inputs), joined(grads_in)
    down_grad = contract_first(all_grads, joined(hiddens)) * full_down.astype(F32)
    lefts, weight_grads = [all_inputs, all_inputs], []
    rights = [(gate_terms, full_gate), (up_terms, full_up)]
    sums = outputs + in_grads
    for bit in range(lax.axis_size("col").bit_length() - 1):
        staged = [col_stage(total, bit) for total in sums]
        if lefts:
            sent, left = lax.optimization_barrier(([s for _, s in staged], lefts.pop()))
            staged = [(kept, s) for (kept, _), s in zip(staged, sent)]
            terms, mask = rights[len(weight_grads)]
            weight_grads.append(contract_first(left, joined(terms)) * mask.astype(F32))
        sums = [col_swap(kept, s, bit) for kept, s in staged]
    for terms, mask in rights[len(weight_grads) :]:
        weight_grads.append(contract_first(all_inputs, joined(terms)) * mask.astype(F32))
    gate_grad, up_grad = weight_grads
    return (joined(sums[:SPLIT]), joined(sums[SPLIT:]), gate_grad, up_grad, down_grad)


def solution(mesh):
    tokens, weights = P(("col", "depth"), "row"), P("row", ("col", "depth"))
    return jax.shard_map(
        per_device,
        mesh=mesh,
        in_specs=(tokens,) * 2 + (weights,) * 6,
        out_specs=(tokens,) * 2 + (weights,) * 3,
        check_vma=False,
    )
```
